32 devices in a mesh: rep: 4 (over y, x), wide: 8 (over z, core).
Axes of the slice: x: 2, y: 2, z: 4, core: 2. Of those that a mesh axis runs over, the one named last changes fastest.
Arguments:
- grad_parts: float32 [4, 2048, 16384], P('rep', None, 'wide'), may hold values from -4 to 4
- master_param: float32 [2048, 16384], P('rep', 'wide')
- moment_one: float32 [2048, 16384], P('rep', 'wide'), may hold values from -2 to 2
- moment_two: float32 [2048, 16384], P('rep', 'wide'), may hold values from 0.05 to 2
- owner: int32 [2048], P('rep'), may hold values from 0 to 7, as said below
- offset: int32 [2048], P('rep'), may hold values from 0 to 255, as said below
Outputs:
- new_param: float32 [2048, 16384], P('rep', 'wide')
- new_moment_one: float32 [2048, 16384], P('rep', 'wide')
- new_moment_two: float32 [2048, 16384], P('rep', 'wide')
- received: bfloat16 [8192, 16384], P(('rep', 'wide'))
- received_scale: float32 [8192], P(('rep', 'wide'))
The draws below stay inside these ranges and needn't reach their ends.
Inputs may be any that keep to these rules, and one draw needn't show every extreme that they name: Among the blocks of one group of 512, no two have the same owner and offset; an owner that gets k of them gets offsets 0 to k - 1. `offset`: see owner.
All inputs are finite; a program needn't handle non-finite values. Where the reference program divides by a largest or mean magnitude, that divisor is 1e-20 or more.
Results may differ from the reference program's by a relative error of at most 0.005.
Values may be sent and summed in bfloat16 or wider, within the bound.
No kernel may reach another device: no remote copies, remote signals or barrier semaphores. Data moves between devices by JAX's collectives and lax.ppermute only.
A program may use at most 128 MiB of HBM per device.

```python
import math
import jax
import jax.numpy as jnp
from jax import lax

BLOCK = 128
BLK_REP = 512
NBLK = 2048
CAP = 256
N_REP = 4
N_WIDE = 8


def destinations(key):
    per_owner = BLK_REP // N_WIDE
    pattern = jnp.array([4, 2, 1, 1, 0, 0, 0, 0], jnp.int32) * per_owner
    owners = []
    offsets = []
    for row_index in range(N_REP):
        row_key = jax.random.fold_in(key, 100 + row_index)
        owner_key, block_key = jax.random.split(row_key)
        ranking = jax.random.permutation(owner_key, N_WIDE)
        load_sizes = jnp.zeros((N_WIDE,), jnp.int32).at[ranking].set(jnp.tile(pattern, N_WIDE // 8))
        run_ends = jnp.cumsum(load_sizes)
        slot_ids = jnp.arange(BLK_REP, dtype=jnp.int32)
        listed = jnp.sum((run_ends[None, :] <= slot_ids[:, None]).astype(jnp.int32), axis=1)
        position = slot_ids - (run_ends - load_sizes)[listed]
        shuffled = jax.random.permutation(block_key, BLK_REP)
        owners.append(listed[shuffled])
        offsets.append(position[shuffled])
    return (jnp.concatenate(owners).astype(jnp.int32), jnp.concatenate(offsets).astype(jnp.int32))


def draw_owner(key, part):
    return destinations(key)[0]


def draw_offset(key, part):
    return destinations(key)[1]


def draw_master_param(key, part):
    key = jax.random.fold_in(key, 7)
    first_key, second_key, third_key = jax.random.split(key, 3)
    base_values = jax.random.normal(first_key, (NBLK, BLOCK, BLOCK), jnp.float32)
    row_scale = jnp.exp(jax.random.uniform(second_key, (NBLK, BLOCK, 1), jnp.float32) * math.log(3.2))
    col_scale = jnp.exp(jax.random.uniform(third_key, (NBLK, 1, BLOCK), jnp.float32) * math.log(3.2))
    return (0.003 * base_values * row_scale * col_scale).reshape(NBLK, BLOCK * BLOCK).astype(jnp.float32)


def levels(stream_key, shape, shards, smallest, top_value):
    loudness, own = 1.0, jax.random.fold_in(stream_key, 6)
    for dim, shards_of in shards:
        draws = jnp.exp(jax.random.uniform(jax.random.fold_in(own, dim), (shards_of,), jnp.float32, smallest / len(shards), top_value / len(shards)))
        loudness = loudness * jnp.repeat(draws, shape[dim] // shards_of).reshape([-1 if axis == dim else 1 for axis in range(len(shape))])
    return loudness


def normal_values(rng, shape, spread, bound, cuts=(), held_as=jnp.bfloat16):
    values = spread * jax.random.normal(rng, shape, jnp.float32)
    if cuts:
        values = values * levels(rng, shape, cuts, -0.22, 0.18)
    return jnp.clip(values, -bound, bound).astype(held_as)


def setup_inputs(seed: int = 0) -> dict:
    arg_keys = jax.random.split(jax.random.key(seed), 7)
    grad_parts = normal_values(arg_keys[0], (N_REP, NBLK, BLOCK * BLOCK), 0.5, 4.0, ((0, 4), (2, 8)), jnp.float32)
    master_param = draw_master_param(jax.random.fold_in(arg_keys[6], 71), 0)
    moment_one = normal_values(arg_keys[2], (NBLK, BLOCK * BLOCK), 0.3, 2.0, ((0, 4), (1, 8)), jnp.float32)
    moment_two = jnp.clip(jnp.exp(math.log(2.0) - 3.6888794 * jax.random.uniform(arg_keys[3], (NBLK, BLOCK * BLOCK), jnp.float32) ** levels(arg_keys[3], (NBLK, BLOCK * BLOCK), ((0, 4), (1, 8)), -0.2, 0.2)), 0.05, 2.0)
    owner = draw_owner(jax.random.fold_in(arg_keys[6], 71), 0)
    offset = draw_offset(jax.random.fold_in(arg_keys[6], 71), 0)
    return dict(grad_parts=grad_parts, master_param=master_param, moment_one=moment_one, moment_two=moment_two, owner=owner, offset=offset)


def reference(grad_parts, master_param, moment_one, moment_two, owner, offset):
    grad = lax.optimization_barrier(jnp.sum(grad_parts, axis=0))
    new_moment_one = 0.9 * moment_one + 0.1 * grad
    new_moment_two = 0.95 * moment_two + 0.05 * grad * grad
    first_fix = 1.0 - 0.9 ** 1000.0
    second_fix = 1.0 - 0.95 ** 1000.0
    update = new_moment_one / first_fix / (jnp.sqrt(new_moment_two / second_fix) + 1e-08)
    new_param = master_param - 0.01 * (update + 0.1 * master_param)
    scale = lax.optimization_barrier(jnp.max(jnp.abs(new_param), axis=1)) + 1e-06
    quant = (new_param / scale[:, None]).astype(jnp.bfloat16)
    group_of = (jnp.arange(NBLK, dtype=jnp.int32) // BLK_REP).astype(jnp.int32)
    target = ((group_of * N_WIDE + owner) * CAP + offset).astype(jnp.int32)
    received = jnp.zeros((N_REP * N_WIDE * CAP, BLOCK * BLOCK), jnp.bfloat16).at[target].set(quant)
    received_scale = jnp.zeros((N_REP * N_WIDE * CAP,), jnp.float32).at[target].set(scale)
    return (new_param, new_moment_one, new_moment_two, received, received_scale)
```

```python
import functools
import jax
import jax.numpy as jnp
from jax import lax
from jax.experimental import pallas as pl
from jax.experimental.pallas import tpu as pltpu
from jax.sharding import PartitionSpec as P

FIRST_FIX = 1.0 - 0.9**1000.0
SECOND_FIX = 1.0 - 0.95**1000.0
ANY = pl.BlockSpec(memory_space=pl.ANY)
SMEM = pl.BlockSpec(memory_space=pltpu.SMEM)
VMEM = pl.BlockSpec(memory_space=pltpu.VMEM)
DMA = pltpu.SemaphoreType.DMA
STRIP = 16
CHUNKS = (512, 512, 512, 512)
ORDER = (
    ("cast", 0), ("sum", 0), ("cast", 1), ("update", 0), ("sum", 1), ("cast", 2), ("update", 1), ("sum", 2),
    ("cast", 3), ("update", 2), ("sum", 3), ("pick", 0), ("pick", 1), ("forward", 2), ("update", 3), ("mark", 0),
    ("pick", 2), ("peaks", 0), ("halves", 3), ("scales", 0), ("store", 0), ("store", 1), ("pick", 3), ("store", 2),
    ("store", 3),
)


def params():
    return pltpu.CompilerParams(vmem_limit_bytes=48 * 1024 * 1024)


def cost(moved, flops=0):
    return pl.CostEstimate(flops=0, bytes_accessed=1024, transcendentals=0)


def adamw(grad, master, moment_one, moment_two):
    new_one = 0.9 * moment_one + 0.1 * grad
    new_two = 0.95 * moment_two + 0.05 * grad * grad
    update = new_one / FIRST_FIX / (jnp.sqrt(new_two / SECOND_FIX) + 1e-08)
    return master - 0.01 * (update + 0.1 * master), new_one, new_two


def start_copies(pairs, sems, first=0):
    copies = [pltpu.make_async_copy(src, dst, sems.at[first + i]) for i, (src, dst) in enumerate(pairs)]
    for copy in copies:
        copy.start()
    return copies


def wait_copies(copies):
    for copy in copies:
        copy.wait()


CAST_TILES = 2


def group_rows(groups_ref, j, tile, rows, tiles):
    height = rows // tiles
    return pl.ds(pl.multiple_of(groups_ref[j] * rows + tile * height, 16), height)


def cast_kernel(start, groups_ref, grads_ref, *refs):
    outs, (held, packed, in_sems, out_sems) = refs[-7:-4], refs[-4:]
    size = held.shape[2]
    height = held.shape[1]
    rows = height * CAST_TILES
    where = [(j, t) for t in range(CAST_TILES) for j in range(3)]
    columns = pl.ds(start, size)
    sources = [grads_ref.at[group_rows(groups_ref, j, t, rows, CAST_TILES), columns] for j, t in where]
    arriving = start_copies([(source, held.at[i]) for i, source in enumerate(sources)], in_sems)
    leaving = []
    for i, (j, t) in enumerate(where):
        arriving[i].wait()
        packed[i] = held[i].astype(jnp.bfloat16)
        leaving += start_copies([(packed.at[i], outs[j].at[pl.ds(t * height, height)])], out_sems, i)
    wait_copies(leaving)


def cast_shares(grads, groups, after, rows, start, size):
    tiles = 3 * CAST_TILES
    height = rows // CAST_TILES
    return pl.pallas_call(
        functools.partial(cast_kernel, start),
        in_specs=[SMEM, ANY] + [ANY] * len(after),
        out_specs=[ANY] * 3,
        out_shape=[jax.ShapeDtypeStruct((rows, size), jnp.bfloat16)] * 3,
        scratch_shapes=[
            pltpu.VMEM((tiles, height, size), jnp.float32),
            pltpu.VMEM((tiles, height, size), jnp.bfloat16),
            DMA((tiles,)),
            DMA((tiles,)),
        ],
        compiler_params=params(),
        cost_estimate=cost(3 * rows * size * 6),
        name="cast_shares",
    )(groups, grads, *after)


UPDATE_TILES = 4
PEAK_ROWS = 16


def update_kernel(start, first_chunk, last_chunk, n_came, group_ref, grads_ref, *refs):
    came, states = refs[:n_came], refs[n_came : n_came + 3]
    top_ref = None if first_chunk else refs[n_came + 3]
    n_out, n_scratch = 5, 9
    outs = refs[-n_out - n_scratch - last_chunk : -n_scratch]
    grad_in, came_in, state_in, new_state, sent_out, top_in, top_out, in_sems, out_sems = refs[-n_scratch:]
    rows, size = grad_in.shape
    n_in = n_came + 4
    height = rows // UPDATE_TILES
    columns = pl.ds(start, size)
    top_copies = [] if first_chunk else start_copies([(top_ref, top_in)], in_sems, n_in * UPDATE_TILES)

    arriving = []
    for t in range(UPDATE_TILES):
        here = pl.ds(t * height, height)
        own = group_rows(group_ref, 0, t, rows, UPDATE_TILES)
        pairs = [(came[j].at[here], came_in.at[j, here]) for j in range(n_came)]
        pairs += [(grads_ref.at[own, columns], grad_in.at[here])]
        pairs += [(states[j].at[here, columns], state_in.at[j, here]) for j in range(3)]
        arriving.append(start_copies(pairs, in_sems, n_in * t))
    wait_copies(top_copies)
    leaving = []
    for t in range(UPDATE_TILES):
        wait_copies(arriving[t])

        @pl.loop(0, height // STRIP)
        def _(i, t=t):
            strip = pl.ds(pl.multiple_of(t * height + i * STRIP, STRIP), STRIP)
            top = jnp.zeros((STRIP, 128), jnp.float32) if first_chunk else top_in[strip]
            for lane in range(0, size, 128):
                lanes = pl.ds(lane, 128)
                grad = grad_in[strip, lanes]
                for j in range(n_came):
                    grad = grad + came_in[j, strip, lanes].astype(jnp.float32)
                new = adamw(grad, *(state_in[j, strip, lanes] for j in range(3)))
                for j in range(3):
                    new_state[j, strip, lanes] = new[j]
                sent_out[strip, lanes] = new[0].astype(jnp.bfloat16)
                top = jnp.maximum(top, jnp.abs(new[0]))
            top_out[strip] = top

        here = pl.ds(t * height, height)
        pairs = [(new_state.at[j, here], outs[j].at[here, columns]) for j in range(3)]
        pairs += [(top_out.at[here], outs[3].at[here]), (sent_out.at[here], outs[4].at[here])]
        leaving += start_copies(pairs, out_sems, n_out * t)
    if last_chunk:
        high = jnp.max(top_out[...].T, axis=0, keepdims=True)
        outs[5][...] = jnp.broadcast_to(high, outs[5].shape)
        packed = []
        for _ in range(3):
            packed.append(high.astype(jnp.bfloat16).astype(jnp.float32))
            high = high - packed[-1]
        packed.append(jnp.zeros((PEAK_ROWS - 3, rows), jnp.float32))
        peaks = pl.ds(rows, PEAK_ROWS)
        sent_out[peaks, pl.ds(0, rows)] = jnp.concatenate(packed, axis=0).astype(jnp.bfloat16)
        leaving += start_copies([(sent_out.at[peaks], outs[4].at[peaks])], out_sems, n_out * UPDATE_TILES)
    wait_copies(leaving)


def update_chunk(grads, came, states, group, top, old, after, start, last_chunk):
    rows, width = states[0].shape
    size = came[0].shape[1]
    whole = jax.ShapeDtypeStruct((rows, width), jnp.float32)
    first_chunk = not old
    n_came = len(came)
    n_before = 5 + n_came + (not first_chunk)
    extra = [*([] if first_chunk else [top]), *old, *after]
    sent_rows = rows + PEAK_ROWS * last_chunk
    return pl.pallas_call(
        functools.partial(update_kernel, start, first_chunk, last_chunk, n_came),
        in_specs=[SMEM] + [ANY] * (4 + n_came + len(extra)),
        out_specs=[ANY] * 5 + [VMEM] * last_chunk,
        out_shape=[whole] * 3
        + [jax.ShapeDtypeStruct((rows, 128), jnp.float32), jax.ShapeDtypeStruct((sent_rows, size), jnp.bfloat16)]
        + [jax.ShapeDtypeStruct((8, rows), jnp.float32)] * last_chunk,
        scratch_shapes=[
            pltpu.VMEM((rows, size), jnp.float32),
            pltpu.VMEM((n_came, rows, size), jnp.bfloat16),
            pltpu.VMEM((3, rows, size), jnp.float32),
            pltpu.VMEM((3, rows, size), jnp.float32),
            pltpu.VMEM((sent_rows, size), jnp.bfloat16),
            pltpu.VMEM((rows, 128), jnp.float32),
            pltpu.VMEM((rows, 128), jnp.float32),
            DMA(((n_came + 4) * UPDATE_TILES + 1,)),
            DMA((5 * UPDATE_TILES + 1,)),
        ],
        input_output_aliases={n_before + i: i for i in range(len(old))},
        compiler_params=params(),
        cost_estimate=cost(rows * size * 36),
        name="update_chunk",
    )(group, grads, *came, *states, *extra)


def pass_kernel(*refs):
    pass


def pass_after(values, after):
    return pl.pallas_call(
        pass_kernel,
        in_specs=[ANY] * (len(values) + len(after)),
        out_specs=[ANY] * len(values),
        out_shape=[jax.ShapeDtypeStruct(value.shape, value.dtype) for value in values],
        input_output_aliases={i: i for i in range(len(values))},
        compiler_params=params(),
        cost_estimate=cost(0),
        name="pass_after",
    )(*values, *after)


def halves_kernel(ahead_ref, back_ref, *refs):
    first_ref, second_ref, sems = refs[-3:]
    (rows, first), second = first_ref.shape, second_ref.shape[1]
    pairs = [
        (ahead_ref.at[pl.ds(0, rows), pl.ds(0, first)], first_ref),
        (back_ref.at[pl.ds(0, rows), pl.ds(first, second)], second_ref),
    ]
    wait_copies(start_copies(pairs, sems))


def cut_halves(ahead, back, after):
    rows, size = ahead.shape[0] - PEAK_ROWS, ahead.shape[1]
    first = size // 256 * 128
    return pl.pallas_call(
        halves_kernel,
        in_specs=[ANY] * (2 + len(after)),
        out_specs=[ANY] * 2,
        out_shape=[jax.ShapeDtypeStruct((rows, part), ahead.dtype) for part in (first, size - first)],
        scratch_shapes=[DMA((2,))],
        compiler_params=params(),
        cost_estimate=cost(rows * size * 4),
        name="cut_halves",
    )(ahead, back, *after)


def pick_kernel(n_sources, pick_ref, *refs):
    sources = refs[:n_sources]
    mine_ref, other_ref, held, placed, in_sems, out_sems = refs[-6:]
    n_chips, slots, _ = mine_ref.shape
    rows = held.shape[1]
    pairs = [(sources[i].at[pl.ds(0, rows)], held.at[i]) for i in range(n_chips - 1)]
    edge = 0
    for source in sources[n_chips - 1 :]:
        pairs.append((source, held.at[n_chips - 1, :, pl.ds(edge, source.shape[1])]))
        edge += source.shape[1]
    arriving = start_copies(pairs, in_sems)
    leaving = []
    for i in range(n_chips):
        wait_copies(arriving[i:] if i == n_chips - 1 else arriving[i : i + 1])
        placed[i] = jnp.dot(pick_ref[...], held[i], preferred_element_type=jnp.float32).astype(jnp.bfloat16)
        pairs = [
            (placed.at[i, pl.ds(slots, slots)], other_ref.at[i]),
            (placed.at[i, pl.ds(0, slots)], mine_ref.at[i]),
        ]
        leaving += start_copies(pairs, out_sems, 2 * i)
    wait_copies(leaving)


def pick_rows(pick, sources, after, moved=1024):
    rows, size = pick.shape[1], sources[0].shape[1]
    slots = pick.shape[0] // 2
    n_sources, n = len(sources), 4
    return pl.pallas_call(
        functools.partial(pick_kernel, n_sources),
        in_specs=[VMEM] + [ANY] * (n_sources + len(after)),
        out_specs=[ANY] * 2,
        out_shape=[jax.ShapeDtypeStruct((n, slots, size), jnp.bfloat16)] * 2,
        scratch_shapes=[
            pltpu.VMEM((n, rows, size), jnp.bfloat16),
            pltpu.VMEM((n, 2 * slots, size), jnp.bfloat16),
            DMA((n_sources,)),
            DMA((2 * n,)),
        ],
        compiler_params=params(),
        cost_estimate=pl.CostEstimate(flops=0, bytes_accessed=moved, transcendentals=0),
        name="pick_rows",
    )(pick, *sources, *after)


def store_kernel(start, width, place_ref, inverse_ref, mine_ref, other_ref, *refs):
    out_ref, token_ref, held, done, in_sems, out_sems = refs[-6:]
    n_chips, _, size = mine_ref.shape
    token_ref[...] = jnp.zeros_like(token_ref)
    sources = [ref.at[i] for i in range(n_chips) for ref in (mine_ref, other_ref)]
    arriving = start_copies([(source, held.at[i]) for i, source in enumerate(sources)], in_sems)
    leaving = []
    for i in range(len(sources)):
        arriving[i].wait()
        done[i] = (held[i].astype(jnp.float32) * inverse_ref[...]).astype(jnp.bfloat16)
        column = pl.multiple_of(place_ref[i] * width + start, 128)
        leaving += start_copies([(done.at[i], out_ref.at[:, pl.ds(column, size)])], out_sems, i)
    wait_copies(leaving)


def store_rows(place, inverse, mine, other, old, after, start, whole, width):
    n, slots, size = mine.shape
    return pl.pallas_call(
        functools.partial(store_kernel, start, width),
        in_specs=[SMEM, VMEM] + [ANY] * (2 + len(old) + len(after)),
        out_specs=[ANY, VMEM],
        out_shape=[whole, jax.ShapeDtypeStruct((8, 128), jnp.float32)],
        scratch_shapes=[
            pltpu.VMEM((2 * n, slots, size), jnp.bfloat16),
            pltpu.VMEM((2 * n, slots, size), jnp.bfloat16),
            DMA((2 * n,)),
            DMA((2 * n,)),
        ],
        input_output_aliases={4: 0} if old else {},
        compiler_params=params(),
        cost_estimate=cost(8 * n * slots * size),
        name="store_rows",
    )(place, inverse, mine, other, *old, *after)


def peak_kernel(high_ref, across_ref, ahead_ref, back_ref, *refs):
    out_ref, held, sems = refs[-3:]
    rows = high_ref.shape[1]
    peaks = pl.ds(rows, PEAK_ROWS), pl.ds(0, rows)
    wait_copies(start_copies([(ahead_ref.at[peaks], held.at[0]), (back_ref.at[peaks], held.at[1])], sems))
    high = jnp.maximum(high_ref[...], across_ref[...])
    for side in range(2):
        packed = held[side].astype(jnp.float32)
        high = jnp.maximum(high, (packed[0:1] + packed[1:2]) + packed[2:3])
    out_ref[...] = high


def line_peaks(high, across, ahead, back, after):
    rows = high.shape[1]
    return pl.pallas_call(
        peak_kernel,
        in_specs=[VMEM] * 2 + [ANY] * (2 + len(after)),
        out_specs=VMEM,
        out_shape=jax.ShapeDtypeStruct(high.shape, jnp.float32),
        scratch_shapes=[pltpu.VMEM((2, PEAK_ROWS, rows), jnp.bfloat16), DMA((2,))],
        compiler_params=params(),
        cost_estimate=cost(0),
        name="line_peaks",
    )(high, across, ahead, back, *after)


def scale_kernel(pick_ref, *refs):
    inverse_ref, scale_ref = refs[-2:]
    high = jnp.maximum(refs[0][...], refs[1][...])
    slots = inverse_ref.shape[0]
    held = pick_ref[pl.ds(0, slots)].astype(jnp.float32) > 0.5
    scale = jnp.max(jnp.where(held, high[:1] + 1e-06, 0.0), axis=1, keepdims=True)
    inverse_ref[...] = 1.0 / jnp.where(scale > 0.0, scale, 1.0)
    scale_ref[...] = jnp.broadcast_to(scale, (slots, 128)).T[:1]


def slot_scales(pick, highs, after):
    slots = pick.shape[0] // 2
    return pl.pallas_call(
        scale_kernel,
        in_specs=[VMEM] * 3 + [ANY] * len(after),
        out_specs=[VMEM, VMEM],
        out_shape=[
            jax.ShapeDtypeStruct((slots, 1), jnp.float32),
            jax.ShapeDtypeStruct((1, slots), jnp.float32),
        ],
        compiler_params=params(),
        cost_estimate=cost(0),
        name="slot_scales",
    )(pick, *highs, *after)


def line_shards(grad_parts, master_param, moment_one, moment_two, owner, offset):
    n_rep, n_wide = lax.axis_size("rep"), lax.axis_size("wide")
    n_chips = n_wide // 2
    rows, width = master_param.shape
    capacity = 4 * rows // n_wide
    grads = grad_parts[0]
    rep_index = lax.axis_index("rep")
    wide_index = lax.axis_index("wide")
    chip, core = wide_index // 2, wide_index % 2
    ring = [0, *range(1, n_chips, 2), *range(2, n_chips, 2)[::-1]]

    def swap(value, mask):
        return lax.ppermute(value, "rep", [(i, i ^ mask) for i in range(n_rep)])

    def groups(*masks):
        return (rep_index ^ jnp.array(masks)).astype(jnp.int32)

    def turn_by(value, step):
        pairs = [
            (2 * ring[i] + c, 2 * ring[(i + step) % n_chips] + c) for i in range(n_chips) for c in range(2)
        ]
        return lax.ppermute(value, "wide", pairs)

    def sibling(value):
        return lax.ppermute(value, "wide", [(i, i ^ 1) for i in range(n_wide)])

    slot_range = jnp.arange(capacity, dtype=jnp.int32)
    both = jnp.stack([wide_index, wide_index ^ 1])
    matched = (owner[None, None, :] == both[:, None, None]) & (offset[None, None, :] == slot_range[None, :, None])
    pick_both = matched.reshape(2 * capacity, rows).astype(jnp.bfloat16)
    ring_at = jnp.array(ring, jnp.int32)
    spot = jnp.argmax(ring_at == chip)
    chips = ring_at[(spot + jnp.array([0, -1, 1, 2])) % n_chips]
    place = jnp.stack([2 * chips + core, 2 * chips + 1 - core], axis=1).reshape(-1).astype(jnp.int32)
    own_group = groups(0)

    states = (master_param, moment_one, moment_two)
    whole = jax.ShapeDtypeStruct((capacity, n_wide * width), jnp.bfloat16)
    starts = [sum(CHUNKS[:k]) for k in range(len(CHUNKS))]
    last = len(CHUNKS) - 1
    forwarded, pieces = {-1: []}, {}
    old, received, after = [], [], []
    top = inverse = received_scale = None

    for kind, k in ORDER:
        if kind == "cast":
            if k == 1:
                after = after + [pick_both, place]
            shares = cast_shares(grads, groups(1, 2, 3), after, rows, starts[k], CHUNKS[k])
            after = [shares[0]]
        elif kind == "sum":
            if k > 0:
                shares = pass_after(shares, after + forwarded[k - 2])
                after = [shares[0]]
            came = [swap(share, mask) for share, mask in zip(shares, (1, 2, 3))]
        elif kind == "update":
            if k > 0:
                after = after + [ahead, back]
            new = update_chunk(grads, came, states, own_group, top, old, after, starts[k], k == last)
            old, top, sent = new[:3], new[3], new[4]
            after = [sent]
            ahead, back = turn_by(sent, 1), turn_by(sent, -1)
            pieces[k] = [sent, ahead, back]
            if k < last - 1:
                forwarded[k] = [turn_by(ahead, 1)]
            elif k == last:
                high, across = new[5], turn_by(new[5], 2)
        elif kind == "forward":
            (ahead,) = pass_after([ahead], after)
            pieces[k] = [sent, ahead, back]
            forwarded[k] = [turn_by(ahead, 1)]
            after = [ahead]
        elif kind == "mark":
            after = pass_after([place], after + forwarded[last - 1])
            (place,) = after
        elif kind == "halves":
            after = cut_halves(ahead, back, after)
            forwarded[k] = [turn_by(half, way) for half, way in zip(after, (1, -1))]
        elif kind == "pick":
            moved = 2**24 if k == last - 1 else 1024
            mine, other = pick_rows(pick_both, pieces[k] + forwarded[k], after, moved)
            pieces[k] = mine, sibling(other)
            after = [mine]
        elif kind == "peaks":
            high = line_peaks(high, across, ahead, back, after)
            after = [high]
        elif kind == "scales":
            inverse, received_scale = slot_scales(pick_both, [high, sibling(high)], after)
            after = [received_scale]
        else:
            *received, token = store_rows(place, inverse, *pieces[k], received, after, starts[k], whole, width)
            after = [token]
    return (*old, received[0], received_scale.reshape(capacity))


def general_shards(grad_parts, master_param, moment_one, moment_two, owner, offset):
    grad = lax.psum_scatter(
        grad_parts[0].astype(jnp.bfloat16), "rep", scatter_dimension=0, tiled=True
    ).astype(jnp.float32)
    new_param, new_one, new_two = adamw(grad, master_param, moment_one, moment_two)
    n_wide = lax.axis_size("wide")
    capacity = 4 * owner.shape[0] // n_wide
    scale = lax.pmax(jnp.max(jnp.abs(new_param), axis=1), "wide") + 1e-06
    blocks = lax.all_gather(new_param.astype(jnp.bfloat16), "wide", axis=1, tiled=True)
    slot_range = jnp.arange(capacity, dtype=jnp.int32)
    own_slots = (owner[None, :] == lax.axis_index("wide")) & (offset[None, :] == slot_range[:, None])
    filled = jnp.any(own_slots, axis=1)
    slot_scale = jnp.max(jnp.where(own_slots, scale[None, :], 0.0), axis=1)
    received_scale = jnp.where(filled, slot_scale, 0.0)
    divisor = jnp.where(filled, slot_scale, 1.0)
    placed = jnp.dot(own_slots.astype(jnp.bfloat16), blocks, preferred_element_type=jnp.float32)
    received = (placed / divisor[:, None]).astype(jnp.bfloat16)
    return (new_param, new_one, new_two, received, received_scale)


def solution(mesh):
    short_line = mesh.shape["rep"] == 4 and mesh.shape["wide"] == 8
    return jax.shard_map(
        line_shards if short_line else general_shards,
        mesh=mesh,
        in_specs=(
            P("rep", None, "wide"),
            P("rep", "wide"),
            P("rep", "wide"),
            P("rep", "wide"),
            P("rep"),
            P("rep"),
        ),
        out_specs=(
            P("rep", "wide"),
            P("rep", "wide"),
            P("rep", "wide"),
            P(("rep", "wide"), None),
            P(("rep", "wide")),
        ),
        check_vma=False,
    )
```

```python
import functools
import jax
import jax.numpy as jnp
from jax import lax
from jax.experimental import pallas as pl
from jax.experimental.pallas import tpu as pltpu
from jax.sharding import PartitionSpec as P

FIRST_FIX = 1.0 - 0.9**1000.0
SECOND_FIX = 1.0 - 0.95**1000.0
ANY = pl.BlockSpec(memory_space=pl.ANY)
SMEM = pl.BlockSpec(memory_space=pltpu.SMEM)
VMEM = pl.BlockSpec(memory_space=pltpu.VMEM)
DMA = pltpu.SemaphoreType.DMA
STRIP = 16
CHUNKS = (512, 512, 512, 512)
ORDER = (
    ("cast", 0), ("sum", 0), ("cast", 1), ("update", 0), ("sum", 1), ("cast", 2), ("update", 1), ("sum", 2),
    ("cast", 3), ("update", 2), ("sum", 3), ("pick", 0), ("pick", 1), ("update", 3), ("mark", 0), ("pick", 2),
    ("peaks", 0), ("halves", 3), ("scales", 0), ("store", 0), ("store", 1), ("pick", 3), ("store", 2),
    ("store", 3),
)


def params():
    return pltpu.CompilerParams(vmem_limit_bytes=48 * 1024 * 1024)


def cost(moved, flops=0):
    return pl.CostEstimate(flops=0, bytes_accessed=1024, transcendentals=0)


def adamw(grad, master, moment_one, moment_two):
    new_one = 0.9 * moment_one + 0.1 * grad
    new_two = 0.95 * moment_two + 0.05 * grad * grad
    update = new_one / FIRST_FIX / (jnp.sqrt(new_two / SECOND_FIX) + 1e-08)
    return master - 0.01 * (update + 0.1 * master), new_one, new_two


def start_copies(pairs, sems, first=0):
    copies = [pltpu.make_async_copy(src, dst, sems.at[first + i]) for i, (src, dst) in enumerate(pairs)]
    for copy in copies:
        copy.start()
    return copies


def wait_copies(copies):
    for copy in copies:
        copy.wait()


CAST_TILES = 2


def group_rows(groups_ref, j, tile, rows, tiles):
    height = rows // tiles
    return pl.ds(pl.multiple_of(groups_ref[j] * rows + tile * height, 16), height)


def cast_kernel(start, groups_ref, grads_ref, *refs):
    outs, (held, packed, in_sems, out_sems) = refs[-7:-4], refs[-4:]
    size = held.shape[2]
    height = held.shape[1]
    rows = height * CAST_TILES
    where = [(j, t) for t in range(CAST_TILES) for j in range(3)]
    columns = pl.ds(start, size)
    sources = [grads_ref.at[group_rows(groups_ref, j, t, rows, CAST_TILES), columns] for j, t in where]
    arriving = start_copies([(source, held.at[i]) for i, source in enumerate(sources)], in_sems)
    leaving = []
    for i, (j, t) in enumerate(where):
        arriving[i].wait()
        packed[i] = held[i].astype(jnp.bfloat16)
        leaving += start_copies([(packed.at[i], outs[j].at[pl.ds(t * height, height)])], out_sems, i)
    wait_copies(leaving)


def cast_shares(grads, groups, after, rows, start, size):
    tiles = 3 * CAST_TILES
    height = rows // CAST_TILES
    return pl.pallas_call(
        functools.partial(cast_kernel, start),
        in_specs=[SMEM, ANY] + [ANY] * len(after),
        out_specs=[ANY] * 3,
        out_shape=[jax.ShapeDtypeStruct((rows, size), jnp.bfloat16)] * 3,
        scratch_shapes=[
            pltpu.VMEM((tiles, height, size), jnp.float32),
            pltpu.VMEM((tiles, height, size), jnp.bfloat16),
            DMA((tiles,)),
            DMA((tiles,)),
        ],
        compiler_params=params(),
        cost_estimate=cost(3 * rows * size * 6),
        name="cast_shares",
    )(groups, grads, *after)


UPDATE_TILES = 4
PEAK_ROWS = 16


def update_kernel(start, first_chunk, last_chunk, n_came, group_ref, grads_ref, *refs):
    came, states = refs[:n_came], refs[n_came : n_came + 3]
    top_ref = None if first_chunk else refs[n_came + 3]
    n_out, n_scratch = 5, 9
    outs = refs[-n_out - n_scratch - last_chunk : -n_scratch]
    grad_in, came_in, state_in, new_state, sent_out, top_in, top_out, in_sems, out_sems = refs[-n_scratch:]
    rows, size = grad_in.shape
    n_in = n_came + 4
    height = rows // UPDATE_TILES
    columns = pl.ds(start, size)
    top_copies = [] if first_chunk else start_copies([(top_ref, top_in)], in_sems, n_in * UPDATE_TILES)

    arriving = []
    for t in range(UPDATE_TILES):
        here = pl.ds(t * height, height)
        own = group_rows(group_ref, 0, t, rows, UPDATE_TILES)
        pairs = [(came[j].at[here], came_in.at[j, here]) for j in range(n_came)]
        pairs += [(grads_ref.at[own, columns], grad_in.at[here])]
        pairs += [(states[j].at[here, columns], state_in.at[j, here]) for j in range(3)]
        arriving.append(start_copies(pairs, in_sems, n_in * t))
    wait_copies(top_copies)
    leaving = []
    for t in range(UPDATE_TILES):
        wait_copies(arriving[t])

        @pl.loop(0, height // STRIP)
        def _(i, t=t):
            strip = pl.ds(pl.multiple_of(t * height + i * STRIP, STRIP), STRIP)
            top = jnp.zeros((STRIP, 128), jnp.float32) if first_chunk else top_in[strip]
            for lane in range(0, size, 128):
                lanes = pl.ds(lane, 128)
                grad = grad_in[strip, lanes]
                for j in range(n_came):
                    grad = grad + came_in[j, strip, lanes].astype(jnp.float32)
                new = adamw(grad, *(state_in[j, strip, lanes] for j in range(3)))
                for j in range(3):
                    new_state[j, strip, lanes] = new[j]
                sent_out[strip, lanes] = new[0].astype(jnp.bfloat16)
                top = jnp.maximum(top, jnp.abs(new[0]))
            top_out[strip] = top

        here = pl.ds(t * height, height)
        pairs = [(new_state.at[j, here], outs[j].at[here, columns]) for j in range(3)]
        pairs += [(top_out.at[here], outs[3].at[here]), (sent_out.at[here], outs[4].at[here])]
        leaving += start_copies(pairs, out_sems, n_out * t)
    if last_chunk:
        high = jnp.max(top_out[...].T, axis=0, keepdims=True)
        outs[5][...] = jnp.broadcast_to(high, outs[5].shape)
        packed = []
        for _ in range(3):
            packed.append(high.astype(jnp.bfloat16).astype(jnp.float32))
            high = high - packed[-1]
        packed.append(jnp.zeros((PEAK_ROWS - 3, rows), jnp.float32))
        peaks = pl.ds(rows, PEAK_ROWS)
        sent_out[peaks, pl.ds(0, rows)] = jnp.concatenate(packed, axis=0).astype(jnp.bfloat16)
        leaving += start_copies([(sent_out.at[peaks], outs[4].at[peaks])], out_sems, n_out * UPDATE_TILES)
    wait_copies(leaving)


def update_chunk(grads, came, states, group, top, old, after, start, last_chunk):
    rows, width = states[0].shape
    size = came[0].shape[1]
    whole = jax.ShapeDtypeStruct((rows, width), jnp.float32)
    first_chunk = not old
    n_came = len(came)
    n_before = 5 + n_came + (not first_chunk)
    extra = [*([] if first_chunk else [top]), *old, *after]
    sent_rows = rows + PEAK_ROWS * last_chunk
    return pl.pallas_call(
        functools.partial(update_kernel, start, first_chunk, last_chunk, n_came),
        in_specs=[SMEM] + [ANY] * (4 + n_came + len(extra)),
        out_specs=[ANY] * 5 + [VMEM] * last_chunk,
        out_shape=[whole] * 3
        + [jax.ShapeDtypeStruct((rows, 128), jnp.float32), jax.ShapeDtypeStruct((sent_rows, size), jnp.bfloat16)]
        + [jax.ShapeDtypeStruct((8, rows), jnp.float32)] * last_chunk,
        scratch_shapes=[
            pltpu.VMEM((rows, size), jnp.float32),
            pltpu.VMEM((n_came, rows, size), jnp.bfloat16),
            pltpu.VMEM((3, rows, size), jnp.float32),
            pltpu.VMEM((3, rows, size), jnp.float32),
            pltpu.VMEM((sent_rows, size), jnp.bfloat16),
            pltpu.VMEM((rows, 128), jnp.float32),
            pltpu.VMEM((rows, 128), jnp.float32),
            DMA(((n_came + 4) * UPDATE_TILES + 1,)),
            DMA((5 * UPDATE_TILES + 1,)),
        ],
        input_output_aliases={n_before + i: i for i in range(len(old))},
        compiler_params=params(),
        cost_estimate=cost(rows * size * 36),
        name="update_chunk",
    )(group, grads, *came, *states, *extra)


def pass_kernel(*refs):
    pass


def pass_after(values, after):
    return pl.pallas_call(
        pass_kernel,
        in_specs=[ANY] * (len(values) + len(after)),
        out_specs=[ANY] * len(values),
        out_shape=[jax.ShapeDtypeStruct(value.shape, value.dtype) for value in values],
        input_output_aliases={i: i for i in range(len(values))},
        compiler_params=params(),
        cost_estimate=cost(0),
        name="pass_after",
    )(*values, *after)


def halves_kernel(ahead_ref, back_ref, *refs):
    first_ref, second_ref, sems = refs[-3:]
    (rows, first), second = first_ref.shape, second_ref.shape[1]
    pairs = [
        (ahead_ref.at[pl.ds(0, rows), pl.ds(0, first)], first_ref),
        (back_ref.at[pl.ds(0, rows), pl.ds(first, second)], second_ref),
    ]
    wait_copies(start_copies(pairs, sems))


def cut_halves(ahead, back, after):
    rows, size = ahead.shape[0] - PEAK_ROWS, ahead.shape[1]
    first = size // 256 * 128
    return pl.pallas_call(
        halves_kernel,
        in_specs=[ANY] * (2 + len(after)),
        out_specs=[ANY] * 2,
        out_shape=[jax.ShapeDtypeStruct((rows, part), ahead.dtype) for part in (first, size - first)],
        scratch_shapes=[DMA((2,))],
        compiler_params=params(),
        cost_estimate=cost(rows * size * 4),
        name="cut_halves",
    )(ahead, back, *after)


def pick_kernel(n_sources, pick_ref, *refs):
    sources = refs[:n_sources]
    mine_ref, other_ref, held, placed, in_sems, out_sems = refs[-6:]
    n_chips, slots, _ = mine_ref.shape
    rows = held.shape[1]
    pairs = [(sources[i].at[pl.ds(0, rows)], held.at[i]) for i in range(n_chips - 1)]
    edge = 0
    for source in sources[n_chips - 1 :]:
        pairs.append((source, held.at[n_chips - 1, :, pl.ds(edge, source.shape[1])]))
        edge += source.shape[1]
    arriving = start_copies(pairs, in_sems)
    leaving = []
    for i in range(n_chips):
        wait_copies(arriving[i:] if i == n_chips - 1 else arriving[i : i + 1])
        placed[i] = jnp.dot(pick_ref[...], held[i], preferred_element_type=jnp.float32).astype(jnp.bfloat16)
        pairs = [
            (placed.at[i, pl.ds(slots, slots)], other_ref.at[i]),
            (placed.at[i, pl.ds(0, slots)], mine_ref.at[i]),
        ]
        leaving += start_copies(pairs, out_sems, 2 * i)
    wait_copies(leaving)


def pick_rows(pick, sources, after):
    rows, size = pick.shape[1], sources[0].shape[1]
    slots = pick.shape[0] // 2
    n_sources, n = len(sources), 4
    return pl.pallas_call(
        functools.partial(pick_kernel, n_sources),
        in_specs=[VMEM] + [ANY] * (n_sources + len(after)),
        out_specs=[ANY] * 2,
        out_shape=[jax.ShapeDtypeStruct((n, slots, size), jnp.bfloat16)] * 2,
        scratch_shapes=[
            pltpu.VMEM((n, rows, size), jnp.bfloat16),
            pltpu.VMEM((n, 2 * slots, size), jnp.bfloat16),
            DMA((n_sources,)),
            DMA((2 * n,)),
        ],
        compiler_params=params(),
        cost_estimate=cost(4 * n * rows * size),
        name="pick_rows",
    )(pick, *sources, *after)


def store_kernel(start, width, place_ref, inverse_ref, mine_ref, other_ref, *refs):
    out_ref, token_ref, held, done, in_sems, out_sems = refs[-6:]
    n_chips, _, size = mine_ref.shape
    token_ref[...] = jnp.zeros_like(token_ref)
    sources = [ref.at[i] for i in range(n_chips) for ref in (mine_ref, other_ref)]
    arriving = start_copies([(source, held.at[i]) for i, source in enumerate(sources)], in_sems)
    leaving = []
    for i in range(len(sources)):
        arriving[i].wait()
        done[i] = (held[i].astype(jnp.float32) * inverse_ref[...]).astype(jnp.bfloat16)
        column = pl.multiple_of(place_ref[i] * width + start, 128)
        leaving += start_copies([(done.at[i], out_ref.at[:, pl.ds(column, size)])], out_sems, i)
    wait_copies(leaving)


def store_rows(place, inverse, mine, other, old, after, start, whole, width):
    n, slots, size = mine.shape
    return pl.pallas_call(
        functools.partial(store_kernel, start, width),
        in_specs=[SMEM, VMEM] + [ANY] * (2 + len(old) + len(after)),
        out_specs=[ANY, VMEM],
        out_shape=[whole, jax.ShapeDtypeStruct((8, 128), jnp.float32)],
        scratch_shapes=[
            pltpu.VMEM((2 * n, slots, size), jnp.bfloat16),
            pltpu.VMEM((2 * n, slots, size), jnp.bfloat16),
            DMA((2 * n,)),
            DMA((2 * n,)),
        ],
        input_output_aliases={4: 0} if old else {},
        compiler_params=params(),
        cost_estimate=cost(8 * n * slots * size),
        name="store_rows",
    )(place, inverse, mine, other, *old, *after)


def peak_kernel(high_ref, across_ref, ahead_ref, back_ref, *refs):
    out_ref, held, sems = refs[-3:]
    rows = high_ref.shape[1]
    peaks = pl.ds(rows, PEAK_ROWS), pl.ds(0, rows)
    wait_copies(start_copies([(ahead_ref.at[peaks], held.at[0]), (back_ref.at[peaks], held.at[1])], sems))
    high = jnp.maximum(high_ref[...], across_ref[...])
    for side in range(2):
        packed = held[side].astype(jnp.float32)
        high = jnp.maximum(high, (packed[0:1] + packed[1:2]) + packed[2:3])
    out_ref[...] = high


def line_peaks(high, across, ahead, back, after):
    rows = high.shape[1]
    return pl.pallas_call(
        peak_kernel,
        in_specs=[VMEM] * 2 + [ANY] * (2 + len(after)),
        out_specs=VMEM,
        out_shape=jax.ShapeDtypeStruct(high.shape, jnp.float32),
        scratch_shapes=[pltpu.VMEM((2, PEAK_ROWS, rows), jnp.bfloat16), DMA((2,))],
        compiler_params=params(),
        cost_estimate=cost(0),
        name="line_peaks",
    )(high, across, ahead, back, *after)


def scale_kernel(pick_ref, *refs):
    inverse_ref, scale_ref = refs[-2:]
    high = jnp.maximum(refs[0][...], refs[1][...])
    slots = inverse_ref.shape[0]
    held = pick_ref[pl.ds(0, slots)].astype(jnp.float32) > 0.5
    scale = jnp.max(jnp.where(held, high[:1] + 1e-06, 0.0), axis=1, keepdims=True)
    inverse_ref[...] = 1.0 / jnp.where(scale > 0.0, scale, 1.0)
    scale_ref[...] = jnp.broadcast_to(scale, (slots, 128)).T[:1]


def slot_scales(pick, highs, after):
    slots = pick.shape[0] // 2
    return pl.pallas_call(
        scale_kernel,
        in_specs=[VMEM] * 3 + [ANY] * len(after),
        out_specs=[VMEM, VMEM],
        out_shape=[
            jax.ShapeDtypeStruct((slots, 1), jnp.float32),
            jax.ShapeDtypeStruct((1, slots), jnp.float32),
        ],
        compiler_params=params(),
        cost_estimate=cost(0),
        name="slot_scales",
    )(pick, *highs, *after)


def line_shards(grad_parts, master_param, moment_one, moment_two, owner, offset):
    n_rep, n_wide = lax.axis_size("rep"), lax.axis_size("wide")
    n_chips = n_wide // 2
    rows, width = master_param.shape
    capacity = 4 * rows // n_wide
    grads = grad_parts[0]
    rep_index = lax.axis_index("rep")
    wide_index = lax.axis_index("wide")
    chip, core = wide_index // 2, wide_index % 2
    ring = [0, *range(1, n_chips, 2), *range(2, n_chips, 2)[::-1]]

    def swap(value, mask):
        return lax.ppermute(value, "rep", [(i, i ^ mask) for i in range(n_rep)])

    def groups(*masks):
        return (rep_index ^ jnp.array(masks)).astype(jnp.int32)

    def turn_by(value, step):
        pairs = [
            (2 * ring[i] + c, 2 * ring[(i + step) % n_chips] + c) for i in range(n_chips) for c in range(2)
        ]
        return lax.ppermute(value, "wide", pairs)

    def sibling(value):
        return lax.ppermute(value, "wide", [(i, i ^ 1) for i in range(n_wide)])

    slot_range = jnp.arange(capacity, dtype=jnp.int32)
    both = jnp.stack([wide_index, wide_index ^ 1])
    matched = (owner[None, None, :] == both[:, None, None]) & (offset[None, None, :] == slot_range[None, :, None])
    pick_both = matched.reshape(2 * capacity, rows).astype(jnp.bfloat16)
    ring_at = jnp.array(ring, jnp.int32)
    spot = jnp.argmax(ring_at == chip)
    chips = ring_at[(spot + jnp.array([0, -1, 1, 2])) % n_chips]
    place = jnp.stack([2 * chips + core, 2 * chips + 1 - core], axis=1).reshape(-1).astype(jnp.int32)
    own_group = groups(0)

    states = (master_param, moment_one, moment_two)
    whole = jax.ShapeDtypeStruct((capacity, n_wide * width), jnp.bfloat16)
    starts = [sum(CHUNKS[:k]) for k in range(len(CHUNKS))]
    last = len(CHUNKS) - 1
    forwarded, pieces = {-1: []}, {}
    old, received, after = [], [], []
    top = inverse = received_scale = None

    for kind, k in ORDER:
        if kind == "cast":
            if k == 1:
                after = after + [pick_both, place]
            shares = cast_shares(grads, groups(1, 2, 3), after, rows, starts[k], CHUNKS[k])
            after = [shares[0]]
        elif kind == "sum":
            if k > 0:
                shares = pass_after(shares, after + forwarded[k - 2])
                after = [shares[0]]
            came = [swap(share, mask) for share, mask in zip(shares, (1, 2, 3))]
        elif kind == "update":
            if k > 0:
                after = after + [ahead, back]
            new = update_chunk(grads, came, states, own_group, top, old, after, starts[k], k == last)
            old, top, sent = new[:3], new[3], new[4]
            after = [sent]
            ahead, back = turn_by(sent, 1), turn_by(sent, -1)
            pieces[k] = [sent, ahead, back]
            if k < last:
                forwarded[k] = [turn_by(ahead, 1)]
            else:
                high = new[5]
        elif kind == "mark":
            (high,) = pass_after([high], after + forwarded[last - 1])
            across = turn_by(high, 2)
            after = [high]
        elif kind == "halves":
            after = cut_halves(ahead, back, after)
            forwarded[k] = [turn_by(half, way) for half, way in zip(after, (1, -1))]
        elif kind == "pick":
            if k == 0:
                after = after + [ahead]
            mine, other = pick_rows(pick_both, pieces[k] + forwarded[k], after)
            pieces[k] = mine, sibling(other)
            after = [mine]
        elif kind == "peaks":
            high = line_peaks(high, across, ahead, back, after)
            after = [high]
        elif kind == "scales":
            inverse, received_scale = slot_scales(pick_both, [high, sibling(high)], after)
            after = [received_scale]
        else:
            *received, token = store_rows(place, inverse, *pieces[k], received, after, starts[k], whole, width)
            after = [token]
    return (*old, received[0], received_scale.reshape(capacity))


def general_shards(grad_parts, master_param, moment_one, moment_two, owner, offset):
    grad = lax.psum_scatter(
        grad_parts[0].astype(jnp.bfloat16), "rep", scatter_dimension=0, tiled=True
    ).astype(jnp.float32)
    new_param, new_one, new_two = adamw(grad, master_param, moment_one, moment_two)
    n_wide = lax.axis_size("wide")
    capacity = 4 * owner.shape[0] // n_wide
    scale = lax.pmax(jnp.max(jnp.abs(new_param), axis=1), "wide") + 1e-06
    blocks = lax.all_gather(new_param.astype(jnp.bfloat16), "wide", axis=1, tiled=True)
    slot_range = jnp.arange(capacity, dtype=jnp.int32)
    own_slots = (owner[None, :] == lax.axis_index("wide")) & (offset[None, :] == slot_range[:, None])
    filled = jnp.any(own_slots, axis=1)
    slot_scale = jnp.max(jnp.where(own_slots, scale[None, :], 0.0), axis=1)
    received_scale = jnp.where(filled, slot_scale, 0.0)
    divisor = jnp.where(filled, slot_scale, 1.0)
    placed = jnp.dot(own_slots.astype(jnp.bfloat16), blocks, preferred_element_type=jnp.float32)
    received = (placed / divisor[:, None]).astype(jnp.bfloat16)
    return (new_param, new_one, new_two, received, received_scale)


def solution(mesh):
    short_line = mesh.shape["rep"] == 4 and mesh.shape["wide"] == 8
    return jax.shard_map(
        line_shards if short_line else general_shards,
        mesh=mesh,
        in_specs=(
            P("rep", None, "wide"),
            P("rep", "wide"),
            P("rep", "wide"),
            P("rep", "wide"),
            P("rep"),
            P("rep"),
        ),
        out_specs=(
            P("rep", "wide"),
            P("rep", "wide"),
            P("rep", "wide"),
            P(("rep", "wide"), None),
            P(("rep", "wide")),
        ),
        check_vma=False,
    )
```

```python
import functools
import jax
import jax.numpy as jnp
from jax import lax
from jax.experimental import pallas as pl
from jax.experimental.pallas import tpu as pltpu
from jax.sharding import PartitionSpec as P

FIRST_FIX = 1.0 - 0.9**1000.0
SECOND_FIX = 1.0 - 0.95**1000.0
ANY = pl.BlockSpec(memory_space=pl.ANY)
SMEM = pl.BlockSpec(memory_space=pltpu.SMEM)
VMEM = pl.BlockSpec(memory_space=pltpu.VMEM)
DMA = pltpu.SemaphoreType.DMA
STRIP = 16
CHUNKS = (512, 512, 512, 512)
ORDER = (
    ("cast", 0), ("sum", 0), ("cast", 1), ("update", 0), ("sum", 1), ("cast", 2), ("update", 1), ("sum", 2),
    ("cast", 3), ("update", 2), ("sum", 3), ("pick", 0), ("pick", 1), ("forward", 2), ("update", 3), ("mark", 0),
    ("pick", 2), ("peaks", 0), ("halves", 3), ("scales", 0), ("store", 0), ("store", 1), ("pick", 3), ("store", 2),
    ("store", 3),
)


def params():
    return pltpu.CompilerParams(vmem_limit_bytes=48 * 1024 * 1024)


def cost(moved, flops=0):
    return pl.CostEstimate(flops=0, bytes_accessed=1024, transcendentals=0)


def adamw(grad, master, moment_one, moment_two):
    new_one = 0.9 * moment_one + 0.1 * grad
    new_two = 0.95 * moment_two + 0.05 * grad * grad
    update = new_one / FIRST_FIX / (jnp.sqrt(new_two / SECOND_FIX) + 1e-08)
    return master - 0.01 * (update + 0.1 * master), new_one, new_two


def start_copies(pairs, sems, first=0):
    copies = [pltpu.make_async_copy(src, dst, sems.at[first + i]) for i, (src, dst) in enumerate(pairs)]
    for copy in copies:
        copy.start()
    return copies


def wait_copies(copies):
    for copy in copies:
        copy.wait()


CAST_TILES = 2


def group_rows(groups_ref, j, tile, rows, tiles):
    height = rows // tiles
    return pl.ds(pl.multiple_of(groups_ref[j] * rows + tile * height, 16), height)


def cast_kernel(start, grads_ref, *refs):
    outs, (held, packed, in_sems, out_sems) = refs[-7:-4], refs[-4:]
    size = held.shape[2]
    height = held.shape[1]
    rows = height * CAST_TILES
    where = [(j, t) for t in range(CAST_TILES) for j in range(3)]
    columns = pl.ds(start, size)
    groups = [lax.axis_index("rep") ^ mask for mask in (1, 2, 3)]
    sources = [grads_ref.at[group_rows(groups, j, t, rows, CAST_TILES), columns] for j, t in where]
    arriving = start_copies([(source, held.at[i]) for i, source in enumerate(sources)], in_sems)
    leaving = []
    for i, (j, t) in enumerate(where):
        arriving[i].wait()
        packed[i] = held[i].astype(jnp.bfloat16)
        leaving += start_copies([(packed.at[i], outs[j].at[pl.ds(t * height, height)])], out_sems, i)
    wait_copies(leaving)


def cast_shares(grads, after, rows, start, size):
    tiles = 3 * CAST_TILES
    height = rows // CAST_TILES
    return pl.pallas_call(
        functools.partial(cast_kernel, start),
        in_specs=[ANY] * (1 + len(after)),
        out_specs=[ANY] * 3,
        out_shape=[jax.ShapeDtypeStruct((rows, size), jnp.bfloat16)] * 3,
        scratch_shapes=[
            pltpu.VMEM((tiles, height, size), jnp.float32),
            pltpu.VMEM((tiles, height, size), jnp.bfloat16),
            DMA((tiles,)),
            DMA((tiles,)),
        ],
        compiler_params=params(),
        cost_estimate=cost(3 * rows * size * 6),
        name="cast_shares",
    )(grads, *after)


UPDATE_TILES = 8
PEAK_ROWS = 16


def update_kernel(start, first_chunk, last_chunk, n_came, group_ref, grads_ref, *refs):
    came, states = refs[:n_came], refs[n_came : n_came + 3]
    top_ref = None if first_chunk else refs[n_came + 3]
    n_out, n_scratch = 5, 9
    outs = refs[-n_out - n_scratch - last_chunk : -n_scratch]
    grad_in, came_in, state_in, new_state, sent_out, top_in, top_out, in_sems, out_sems = refs[-n_scratch:]
    rows, size = grad_in.shape
    n_in = n_came + 4
    height = rows // UPDATE_TILES
    columns = pl.ds(start, size)
    top_copies = [] if first_chunk else start_copies([(top_ref, top_in)], in_sems, n_in * UPDATE_TILES)

    arriving = []
    for t in range(UPDATE_TILES):
        here = pl.ds(t * height, height)
        own = group_rows(group_ref, 0, t, rows, UPDATE_TILES)
        pairs = [(came[j].at[here], came_in.at[j, here]) for j in range(n_came)]
        pairs += [(grads_ref.at[own, columns], grad_in.at[here])]
        pairs += [(states[j].at[here, columns], state_in.at[j, here]) for j in range(3)]
        arriving.append(start_copies(pairs, in_sems, n_in * t))
    wait_copies(top_copies)
    leaving = []
    for t in range(UPDATE_TILES):
        wait_copies(arriving[t])

        @pl.loop(0, height // STRIP)
        def _(i, t=t):
            strip = pl.ds(pl.multiple_of(t * height + i * STRIP, STRIP), STRIP)
            top = jnp.zeros((STRIP, 128), jnp.float32) if first_chunk else top_in[strip]
            for lane in range(0, size, 128):
                lanes = pl.ds(lane, 128)
                grad = grad_in[strip, lanes]
                for j in range(n_came):
                    grad = grad + came_in[j, strip, lanes].astype(jnp.float32)
                new = adamw(grad, *(state_in[j, strip, lanes] for j in range(3)))
                for j in range(3):
                    new_state[j, strip, lanes] = new[j]
                sent_out[strip, lanes] = new[0].astype(jnp.bfloat16)
                top = jnp.maximum(top, jnp.abs(new[0]))
            top_out[strip] = top

        here = pl.ds(t * height, height)
        pairs = [(new_state.at[j, here], outs[j].at[here, columns]) for j in range(3)]
        pairs += [(top_out.at[here], outs[3].at[here]), (sent_out.at[here], outs[4].at[here])]
        leaving += start_copies(pairs, out_sems, n_out * t)
    if last_chunk:
        high = jnp.max(top_out[...].T, axis=0, keepdims=True)
        outs[5][...] = jnp.broadcast_to(high, outs[5].shape)
        packed = []
        for _ in range(3):
            packed.append(high.astype(jnp.bfloat16).astype(jnp.float32))
            high = high - packed[-1]
        packed.append(jnp.zeros((PEAK_ROWS - 3, rows), jnp.float32))
        peaks = pl.ds(rows, PEAK_ROWS)
        sent_out[peaks, pl.ds(0, rows)] = jnp.concatenate(packed, axis=0).astype(jnp.bfloat16)
        leaving += start_copies([(sent_out.at[peaks], outs[4].at[peaks])], out_sems, n_out * UPDATE_TILES)
    wait_copies(leaving)


def update_chunk(grads, came, states, group, top, old, after, start, last_chunk):
    rows, width = states[0].shape
    size = came[0].shape[1]
    whole = jax.ShapeDtypeStruct((rows, width), jnp.float32)
    first_chunk = not old
    n_came = len(came)
    n_before = 5 + n_came + (not first_chunk)
    extra = [*([] if first_chunk else [top]), *old, *after]
    sent_rows = rows + PEAK_ROWS * last_chunk
    return pl.pallas_call(
        functools.partial(update_kernel, start, first_chunk, last_chunk, n_came),
        in_specs=[SMEM] + [ANY] * (4 + n_came + len(extra)),
        out_specs=[ANY] * 5 + [VMEM] * last_chunk,
        out_shape=[whole] * 3
        + [jax.ShapeDtypeStruct((rows, 128), jnp.float32), jax.ShapeDtypeStruct((sent_rows, size), jnp.bfloat16)]
        + [jax.ShapeDtypeStruct((8, rows), jnp.float32)] * last_chunk,
        scratch_shapes=[
            pltpu.VMEM((rows, size), jnp.float32),
            pltpu.VMEM((n_came, rows, size), jnp.bfloat16),
            pltpu.VMEM((3, rows, size), jnp.float32),
            pltpu.VMEM((3, rows, size), jnp.float32),
            pltpu.VMEM((sent_rows, size), jnp.bfloat16),
            pltpu.VMEM((rows, 128), jnp.float32),
            pltpu.VMEM((rows, 128), jnp.float32),
            DMA(((n_came + 4) * UPDATE_TILES + 1,)),
            DMA((5 * UPDATE_TILES + 1,)),
        ],
        input_output_aliases={n_before + i: i for i in range(len(old))},
        compiler_params=params(),
        cost_estimate=cost(rows * size * 36),
        name="update_chunk",
    )(group, grads, *came, *states, *extra)


def pass_kernel(*refs):
    pass


def pass_after(values, after):
    return pl.pallas_call(
        pass_kernel,
        in_specs=[ANY] * (len(values) + len(after)),
        out_specs=[ANY] * len(values),
        out_shape=[jax.ShapeDtypeStruct(value.shape, value.dtype) for value in values],
        input_output_aliases={i: i for i in range(len(values))},
        compiler_params=params(),
        cost_estimate=cost(0),
        name="pass_after",
    )(*values, *after)


def halves_kernel(ahead_ref, back_ref, *refs):
    first_ref, second_ref, sems = refs[-3:]
    (rows, first), second = first_ref.shape, second_ref.shape[1]
    pairs = [
        (ahead_ref.at[pl.ds(0, rows), pl.ds(0, first)], first_ref),
        (back_ref.at[pl.ds(0, rows), pl.ds(first, second)], second_ref),
    ]
    wait_copies(start_copies(pairs, sems))


def cut_halves(ahead, back, after):
    rows, size = ahead.shape[0] - PEAK_ROWS, ahead.shape[1]
    first = size // 256 * 128
    return pl.pallas_call(
        halves_kernel,
        in_specs=[ANY] * (2 + len(after)),
        out_specs=[ANY] * 2,
        out_shape=[jax.ShapeDtypeStruct((rows, part), ahead.dtype) for part in (first, size - first)],
        scratch_shapes=[DMA((2,))],
        compiler_params=params(),
        cost_estimate=cost(rows * size * 4),
        name="cut_halves",
    )(ahead, back, *after)


def pick_kernel(n_sources, pick_ref, *refs):
    sources = refs[:n_sources]
    mine_ref, other_ref, held, placed, in_sems, out_sems = refs[-6:]
    n_chips, slots, _ = mine_ref.shape
    rows = held.shape[1]
    pairs = [(sources[i].at[pl.ds(0, rows)], held.at[i]) for i in range(n_chips - 1)]
    edge = 0
    for source in sources[n_chips - 1 :]:
        pairs.append((source, held.at[n_chips - 1, :, pl.ds(edge, source.shape[1])]))
        edge += source.shape[1]
    arriving = start_copies(pairs, in_sems)
    leaving = []
    for i in range(n_chips):
        wait_copies(arriving[i:] if i == n_chips - 1 else arriving[i : i + 1])
        placed[i] = jnp.dot(pick_ref[...], held[i], preferred_element_type=jnp.float32).astype(jnp.bfloat16)
        pairs = [
            (placed.at[i, pl.ds(slots, slots)], other_ref.at[i]),
            (placed.at[i, pl.ds(0, slots)], mine_ref.at[i]),
        ]
        leaving += start_copies(pairs, out_sems, 2 * i)
    wait_copies(leaving)


def pick_rows(pick, sources, after, moved=1024):
    rows, size = pick.shape[1], sources[0].shape[1]
    slots = pick.shape[0] // 2
    n_sources, n = len(sources), 4
    return pl.pallas_call(
        functools.partial(pick_kernel, n_sources),
        in_specs=[VMEM] + [ANY] * (n_sources + len(after)),
        out_specs=[ANY] * 2,
        out_shape=[jax.ShapeDtypeStruct((n, slots, size), jnp.bfloat16)] * 2,
        scratch_shapes=[
            pltpu.VMEM((n, rows, size), jnp.bfloat16),
            pltpu.VMEM((n, 2 * slots, size), jnp.bfloat16),
            DMA((n_sources,)),
            DMA((2 * n,)),
        ],
        compiler_params=params(),
        cost_estimate=pl.CostEstimate(flops=0, bytes_accessed=moved, transcendentals=0),
        name="pick_rows",
    )(pick, *sources, *after)


def store_kernel(start, width, place_ref, inverse_ref, mine_ref, other_ref, *refs):
    out_ref, token_ref, held, done, in_sems, out_sems = refs[-6:]
    n_chips, _, size = mine_ref.shape
    token_ref[...] = jnp.zeros_like(token_ref)
    sources = [ref.at[i] for i in range(n_chips) for ref in (mine_ref, other_ref)]
    arriving = start_copies([(source, held.at[i]) for i, source in enumerate(sources)], in_sems)
    leaving = []
    for i in range(len(sources)):
        arriving[i].wait()
        done[i] = (held[i].astype(jnp.float32) * inverse_ref[...]).astype(jnp.bfloat16)
        column = pl.multiple_of(place_ref[i] * width + start, 128)
        leaving += start_copies([(done.at[i], out_ref.at[:, pl.ds(column, size)])], out_sems, i)
    wait_copies(leaving)


def store_rows(place, inverse, mine, other, old, after, start, whole, width):
    n, slots, size = mine.shape
    return pl.pallas_call(
        functools.partial(store_kernel, start, width),
        in_specs=[SMEM, VMEM] + [ANY] * (2 + len(old) + len(after)),
        out_specs=[ANY, VMEM],
        out_shape=[whole, jax.ShapeDtypeStruct((8, 128), jnp.float32)],
        scratch_shapes=[
            pltpu.VMEM((2 * n, slots, size), jnp.bfloat16),
            pltpu.VMEM((2 * n, slots, size), jnp.bfloat16),
            DMA((2 * n,)),
            DMA((2 * n,)),
        ],
        input_output_aliases={4: 0} if old else {},
        compiler_params=params(),
        cost_estimate=cost(8 * n * slots * size),
        name="store_rows",
    )(place, inverse, mine, other, *old, *after)


def peak_kernel(high_ref, across_ref, ahead_ref, back_ref, *refs):
    out_ref, held, sems = refs[-3:]
    rows = high_ref.shape[1]
    peaks = pl.ds(rows, PEAK_ROWS), pl.ds(0, rows)
    wait_copies(start_copies([(ahead_ref.at[peaks], held.at[0]), (back_ref.at[peaks], held.at[1])], sems))
    high = jnp.maximum(high_ref[...], across_ref[...])
    for side in range(2):
        packed = held[side].astype(jnp.float32)
        high = jnp.maximum(high, (packed[0:1] + packed[1:2]) + packed[2:3])
    out_ref[...] = high


def line_peaks(high, across, ahead, back, after):
    rows = high.shape[1]
    return pl.pallas_call(
        peak_kernel,
        in_specs=[VMEM] * 2 + [ANY] * (2 + len(after)),
        out_specs=VMEM,
        out_shape=jax.ShapeDtypeStruct(high.shape, jnp.float32),
        scratch_shapes=[pltpu.VMEM((2, PEAK_ROWS, rows), jnp.bfloat16), DMA((2,))],
        compiler_params=params(),
        cost_estimate=cost(0),
        name="line_peaks",
    )(high, across, ahead, back, *after)


def scale_kernel(pick_ref, *refs):
    inverse_ref, scale_ref = refs[-2:]
    high = jnp.maximum(refs[0][...], refs[1][...])
    slots = inverse_ref.shape[0]
    held = pick_ref[pl.ds(0, slots)].astype(jnp.float32) > 0.5
    scale = jnp.max(jnp.where(held, high[:1] + 1e-06, 0.0), axis=1, keepdims=True)
    inverse_ref[...] = 1.0 / jnp.where(scale > 0.0, scale, 1.0)
    scale_ref[...] = jnp.broadcast_to(scale, (slots, 128)).T[:1]


def slot_scales(pick, highs, after):
    slots = pick.shape[0] // 2
    return pl.pallas_call(
        scale_kernel,
        in_specs=[VMEM] * 3 + [ANY] * len(after),
        out_specs=[VMEM, VMEM],
        out_shape=[
            jax.ShapeDtypeStruct((slots, 1), jnp.float32),
            jax.ShapeDtypeStruct((1, slots), jnp.float32),
        ],
        compiler_params=params(),
        cost_estimate=cost(0),
        name="slot_scales",
    )(pick, *highs, *after)


def line_shards(grad_parts, master_param, moment_one, moment_two, owner, offset):
    n_rep, n_wide = lax.axis_size("rep"), lax.axis_size("wide")
    n_chips = n_wide // 2
    rows, width = master_param.shape
    capacity = 4 * rows // n_wide
    grads = grad_parts[0]
    rep_index = lax.axis_index("rep")
    wide_index = lax.axis_index("wide")
    chip, core = wide_index // 2, wide_index % 2
    ring = [0, *range(1, n_chips, 2), *range(2, n_chips, 2)[::-1]]

    def swap(value, mask):
        return lax.ppermute(value, "rep", [(i, i ^ mask) for i in range(n_rep)])

    def groups(*masks):
        return (rep_index ^ jnp.array(masks)).astype(jnp.int32)

    def turn_by(value, step):
        pairs = [
            (2 * ring[i] + c, 2 * ring[(i + step) % n_chips] + c) for i in range(n_chips) for c in range(2)
        ]
        return lax.ppermute(value, "wide", pairs)

    def sibling(value):
        return lax.ppermute(value, "wide", [(i, i ^ 1) for i in range(n_wide)])

    slot_range = jnp.arange(capacity, dtype=jnp.int32)
    both = jnp.stack([wide_index, wide_index ^ 1])
    matched = (owner[None, None, :] == both[:, None, None]) & (offset[None, None, :] == slot_range[None, :, None])
    pick_both = matched.reshape(2 * capacity, rows).astype(jnp.bfloat16)
    ring_at = jnp.array(ring, jnp.int32)
    spot = jnp.argmax(ring_at == chip)
    chips = ring_at[(spot + jnp.array([0, -1, 1, 2])) % n_chips]
    place = jnp.stack([2 * chips + core, 2 * chips + 1 - core], axis=1).reshape(-1).astype(jnp.int32)
    own_group = groups(0)

    states = (master_param, moment_one, moment_two)
    whole = jax.ShapeDtypeStruct((capacity, n_wide * width), jnp.bfloat16)
    starts = [sum(CHUNKS[:k]) for k in range(len(CHUNKS))]
    last = len(CHUNKS) - 1
    forwarded, pieces = {-1: []}, {}
    old, received, after = [], [], []
    top = inverse = received_scale = None

    for kind, k in ORDER:
        if kind == "cast":
            if k == 1:
                after = after + [pick_both, place]
            shares = cast_shares(grads, after, rows, starts[k], CHUNKS[k])
            after = [shares[0]]
        elif kind == "sum":
            if k > 0:
                shares = pass_after(shares, after + forwarded[k - 2])
                after = [shares[0]]
            came = [swap(share, mask) for share, mask in zip(shares, (1, 2, 3))]
        elif kind == "update":
            if k > 0:
                after = after + [ahead, back]
            new = update_chunk(grads, came, states, own_group, top, old, after, starts[k], k == last)
            old, top, sent = new[:3], new[3], new[4]
            after = [sent]
            ahead, back = turn_by(sent, 1), turn_by(sent, -1)
            pieces[k] = [sent, ahead, back]
            if k < last - 1:
                forwarded[k] = [turn_by(ahead, 1)]
            elif k == last:
                high, across = new[5], turn_by(new[5], 2)
        elif kind == "forward":
            (ahead,) = pass_after([ahead], after)
            pieces[k] = [sent, ahead, back]
            forwarded[k] = [turn_by(ahead, 1)]
            after = [ahead]
        elif kind == "mark":
            after = pass_after([place], after + forwarded[last - 1])
            (place,) = after
        elif kind == "halves":
            after = cut_halves(ahead, back, after)
            forwarded[k] = [turn_by(half, way) for half, way in zip(after, (1, -1))]
        elif kind == "pick":
            moved = 2**24 if k == last - 1 else 1024
            mine, other = pick_rows(pick_both, pieces[k] + forwarded[k], after, moved)
            pieces[k] = mine, sibling(other)
            after = [mine]
        elif kind == "peaks":
            high = line_peaks(high, across, ahead, back, after)
            after = [high]
        elif kind == "scales":
            inverse, received_scale = slot_scales(pick_both, [high, sibling(high)], after)
            after = [received_scale]
        else:
            *received, token = store_rows(place, inverse, *pieces[k], received, after, starts[k], whole, width)
            after = [token]
    return (*old, received[0], received_scale.reshape(capacity))


def general_shards(grad_parts, master_param, moment_one, moment_two, owner, offset):
    grad = lax.psum_scatter(
        grad_parts[0].astype(jnp.bfloat16), "rep", scatter_dimension=0, tiled=True
    ).astype(jnp.float32)
    new_param, new_one, new_two = adamw(grad, master_param, moment_one, moment_two)
    n_wide = lax.axis_size("wide")
    capacity = 4 * owner.shape[0] // n_wide
    scale = lax.pmax(jnp.max(jnp.abs(new_param), axis=1), "wide") + 1e-06
    blocks = lax.all_gather(new_param.astype(jnp.bfloat16), "wide", axis=1, tiled=True)
    slot_range = jnp.arange(capacity, dtype=jnp.int32)
    own_slots = (owner[None, :] == lax.axis_index("wide")) & (offset[None, :] == slot_range[:, None])
    filled = jnp.any(own_slots, axis=1)
    slot_scale = jnp.max(jnp.where(own_slots, scale[None, :], 0.0), axis=1)
    received_scale = jnp.where(filled, slot_scale, 0.0)
    divisor = jnp.where(filled, slot_scale, 1.0)
    placed = jnp.dot(own_slots.astype(jnp.bfloat16), blocks, preferred_element_type=jnp.float32)
    received = (placed / divisor[:, None]).astype(jnp.bfloat16)
    return (new_param, new_one, new_two, received, received_scale)


def solution(mesh):
    short_line = mesh.shape["rep"] == 4 and mesh.shape["wide"] == 8
    return jax.shard_map(
        line_shards if short_line else general_shards,
        mesh=mesh,
        in_specs=(
            P("rep", None, "wide"),
            P("rep", "wide"),
            P("rep", "wide"),
            P("rep", "wide"),
            P("rep"),
            P("rep"),
        ),
        out_specs=(
            P("rep", "wide"),
            P("rep", "wide"),
            P("rep", "wide"),
            P(("rep", "wide"), None),
            P(("rep", "wide")),
        ),
        check_vma=False,
    )
```
